32 devices in a mesh: row: 2 (over x), col: 4 (over y, core), feat: 4 (over z).
Axes of the slice: x: 2, y: 2, z: 4, core: 2. Of those that a mesh axis runs over, the one named last changes fastest.
Arguments:
- features: bfloat16 [65536, 128], P(('row', 'col'), 'feat'), may hold values from -6 to 6
- tiles: bfloat16 [2, 4, 1536, 128, 128], P('row', 'col', 'feat'), may hold values from 0 to 0.04321289
- tile_row: int32 [2, 4, 1536], P('row', 'col', 'feat'), may hold values from 0 to 255
- tile_col: int32 [2, 4, 1536], P('row', 'col', 'feat'), may hold values from 0 to 127
- tile_count: int32 [2, 4, 4], P('row', 'col', 'feat'), may hold values from 1 to 384, as said below
- weight: bfloat16 [128, 256], replicated, may hold values from -0.5 to 0.5
- bias: float32 [256], replicated, may hold values from -3 to 3
Outputs:
- output: bfloat16 [65536, 256], P(('row', 'col', 'feat'))
The draws below stay inside these ranges and needn't reach their ends.
Inputs may be any that keep to these rules, and one draw needn't show every extreme that they name: `tile_count`: some device has all 384 slots live.
All inputs are finite; a program needn't handle non-finite values.
Results may differ from the reference program's by a relative error of at most 0.02.
Values may be sent and summed in bfloat16 or wider, within the bound.
A program may use at most 128 MiB of HBM per device.

```python
import math
import jax
import jax.numpy as jnp
import numpy as np
from jax import lax

F = 128
H = 256
TB = 128
NODE_DEV = 2048
TILES_DEV = 384
NODES = 65536
BROWS = 256
BCOLS = 128
SLOTS = 1536
N_ROW = 2
N_COL = 4
N_FEAT = 4


def draw_tile_count(key, part):
    levels = jax.random.randint(key, (N_ROW * N_COL * N_FEAT,), 1, 5)
    counts = jnp.maximum(1, TILES_DEV * levels * levels // 16)
    chosen = jax.random.randint(jax.random.fold_in(key, 7), (), 0, N_ROW * N_COL * N_FEAT)
    counts = counts.at[chosen].set(TILES_DEV)
    return counts.reshape(N_ROW, N_COL, N_FEAT).astype(jnp.int32)


def with_ends(result, stream_key, low, high):
    spot = [jax.random.randint(jax.random.fold_in(stream_key, axis), (), 0, length) for axis, length in enumerate(result.shape)]
    main_axis = result.shape.index(max(result.shape))
    neighbour = spot[:main_axis] + [(spot[main_axis] + 1) % result.shape[main_axis]] + spot[main_axis + 1:]
    return result.at[tuple(spot)].set(low).at[tuple(neighbour)].set(high)


def level_of(stream_key, extent, pieces, least, top_value):
    gain, own = 1.0, jax.random.fold_in(stream_key, 6)
    for axis_at, blocks in pieces:
        draws = jnp.exp(jax.random.uniform(jax.random.fold_in(own, axis_at), (blocks,), jnp.float32, least / len(pieces), top_value / len(pieces)))
        gain = gain * jnp.repeat(draws, extent[axis_at] // blocks).reshape([-1 if axis == axis_at else 1 for axis in range(len(extent))])
    return gain


def rank_bounds(amount, lean):
    loads = [(1 << 20) // math.isqrt(grade ** lean) + 1 for grade in range(1, amount + 1)]
    width = 1 + sum(loads) // (1 << 30)
    return np.cumsum(np.array([max(1, weight // width) for weight in loads]))


def ranked_ids(own_key, shape, amount, skew):
    listing = rank_bounds(amount, skew)
    pick = jax.random.randint(jax.random.fold_in(own_key, 1), shape, 0, int(listing[amount - 1]))
    grade = jnp.searchsorted(jnp.asarray(listing, jnp.int32), pick, side="right")
    return jax.random.permutation(jax.random.fold_in(own_key, 2), amount)[grade].astype(jnp.int32)


def centred(key, extent, spread, limit, cuts=(), kind=jnp.bfloat16):
    array = spread * jax.random.normal(key, extent, jnp.float32)
    if cuts:
        array = array * level_of(key, extent, cuts, -0.22, 0.18)
    return jnp.clip(array, -limit, limit).astype(kind)


def setup_inputs(seed: int = 0) -> dict:
    key_of = jax.random.split(jax.random.key(seed), 8)
    return {
        "features": centred(key_of[0], (NODES, F), 1.0, 6.0, ((0, 8), (1, 4))),
        "tiles": jnp.clip(0.04321289 * jax.random.uniform(key_of[1], (N_ROW, N_COL, SLOTS, TB, TB), jnp.float32) ** level_of(key_of[1], (N_ROW, N_COL, SLOTS, TB, TB), ((0, 2), (1, 4), (2, 4)), -0.2, 0.2), 0.0, 0.04321289).astype(jnp.bfloat16),
        "tile_row": with_ends(ranked_ids(key_of[2], (N_ROW, N_COL, SLOTS), BROWS, 2), jax.random.fold_in(key_of[2], 3), 0, BROWS - 1).astype(jnp.int32),
        "tile_col": with_ends(jax.random.randint(key_of[3], (N_ROW, N_COL, SLOTS), 0, BCOLS), jax.random.fold_in(key_of[3], 1), 0, BCOLS - 1).astype(jnp.int32),
        "tile_count": draw_tile_count(jax.random.fold_in(key_of[7], 71), 0),
        "weight": centred(key_of[5], (F, H), F ** -0.5, 0.5),
        "bias": centred(key_of[6], (H,), 0.5, 3.0, (), jnp.float32),
    }


def device_partial(tile_set, rows, cols, count, src_blocks):
    picked = src_blocks[cols]
    prods = jnp.einsum("tij,tjf->tif", tile_set.astype(jnp.float32), picked.astype(jnp.float32))
    live = jnp.arange(tile_set.shape[0], dtype=jnp.int32) < count
    prods = jnp.where(live[:, None, None], prods, jnp.zeros_like(prods))
    partial_value = jnp.zeros((BROWS, TB, F), jnp.float32).at[rows].add(prods)
    return partial_value.reshape(BROWS * TB, F).astype(jnp.bfloat16)


def reference(features, tiles, tile_row, tile_col, tile_count, weight, bias):
    group = N_FEAT * NODE_DEV
    col_sources = features.reshape(N_ROW, N_COL, group, F).transpose(1, 0, 2, 3).reshape(N_COL, BCOLS, TB, F)
    devs = N_ROW * N_COL * N_FEAT
    tile_all = tiles.reshape(devs, TILES_DEV, TB, TB)
    rows_all = tile_row.reshape(devs, TILES_DEV)
    cols_all = tile_col.reshape(devs, TILES_DEV)
    counts = tile_count.reshape(devs)

    def one_device(index):
        column = (index // N_FEAT) % N_COL
        return device_partial(tile_all[index], rows_all[index], cols_all[index], counts[index], col_sources[column])

    partials = lax.map(one_device, jnp.arange(devs, dtype=jnp.int32))
    agg = partials.astype(jnp.float32).reshape(N_ROW, N_COL * N_FEAT, BROWS * TB, F).sum(axis=1).reshape(NODES, F)
    hidden = jnp.dot(agg.astype(jnp.bfloat16), weight, preferred_element_type=jnp.float32) + bias
    return jax.nn.relu(hidden).astype(jnp.bfloat16)
```

```python
import functools

import jax
import jax.numpy as jnp
from jax import lax
from jax.experimental import pallas as pl
from jax.experimental.pallas import tpu as pltpu
from jax.sharding import PartitionSpec as P

MESH = pl.DeviceIdType.MESH
MIB = 1 << 20


def gather_kernel(n_row, n_feat, parts, own_ref, out_ref, local_sem, z_send, z_recv, x_send, x_recv):
    r = lax.axis_index("row")
    f = lax.axis_index("feat")
    blocks, width = own_ref.shape[0], own_ref.shape[1]
    step = blocks // parts

    barrier = pltpu.get_barrier_semaphore()
    for p in range(1, n_row):
        pl.semaphore_signal(barrier, inc=1, device_id={"row": lax.rem(r + p, n_row)}, device_id_type=MESH)

    @pl.when(f > 0)
    def _():
        pl.semaphore_signal(barrier, inc=1, device_id={"feat": f - 1}, device_id_type=MESH)

    @pl.when(f < n_feat - 1)
    def _():
        pl.semaphore_signal(barrier, inc=1, device_id={"feat": f + 1}, device_id_type=MESH)

    ends = jnp.where(f > 0, 1, 0) + jnp.where(f < n_feat - 1, 1, 0)
    pl.semaphore_wait(barrier, n_row - 1 + ends)

    def region(row, feat, c):
        return out_ref.at[pl.ds(row * blocks + c * step, step), pl.ds(pl.multiple_of(feat * width, width), width), :]

    def own(c):
        return own_ref.at[pl.ds(c * step, step)]

    def along(way, hop, c, origin, src=None):
        target = f + 1 if way == 0 else f - 1
        place = region(r, origin, c)
        return pltpu.make_async_remote_copy(
            src_ref=place if src is None else src, dst_ref=place,
            send_sem=z_send.at[way, hop, c], recv_sem=z_recv.at[way, hop, c],
            device_id={"feat": target}, device_id_type=MESH)

    def across(p, origin, c, src=None):
        place = region(r, origin, c)
        return pltpu.make_async_remote_copy(
            src_ref=place if src is None else src, dst_ref=place,
            send_sem=x_send.at[p - 1, origin, c], recv_sem=x_recv.at[p - 1, origin, c],
            device_id={"row": lax.rem(r + p, n_row)}, device_id_type=MESH)

    for c in range(parts):
        @pl.when(f < n_feat - 1)
        def _():
            along(0, 0, c, f, own(c)).start()

        @pl.when(f > 0)
        def _():
            along(1, 0, c, f, own(c)).start()

        for p in range(1, n_row):
            across(p, f, c, own(c)).start()
    local = pltpu.make_async_copy(own_ref, out_ref.at[pl.ds(r * blocks, blocks), pl.ds(pl.multiple_of(f * width, width), width), :], local_sem)
    local.start()

    for hop in range(1, n_feat):
        for c in range(parts):
            @pl.when(f - hop >= 0)
            def _():
                origin = f - hop
                along(0, hop - 1, c, origin).wait_recv()
                if hop < n_feat - 1:
                    @pl.when(f < n_feat - 1)
                    def _():
                        along(0, hop, c, origin).start()
                for p in range(1, n_row):
                    across(p, origin, c).start()

            @pl.when(f + hop < n_feat)
            def _():
                origin = f + hop
                along(1, hop - 1, c, origin).wait_recv()
                if hop < n_feat - 1:
                    @pl.when(f > 0)
                    def _():
                        along(1, hop, c, origin).start()
                for p in range(1, n_row):
                    across(p, origin, c).start()

    for origin in range(n_feat):
        for c in range(parts):
            for p in range(1, n_row):
                across(p, origin, c).wait()
    for hop in range(n_feat - 1):
        for c in range(parts):
            @pl.when((f < n_feat - 1) & (f - hop >= 0))
            def _():
                along(0, hop, c, f - hop).wait_send()

            @pl.when((f > 0) & (f + hop < n_feat))
            def _():
                along(1, hop, c, f + hop).wait_send()
    local.wait()


def tile_kernel(chunk, unroll, brows, count_ref, row_ref, col_ref, src_ref, tiles_ref, out_ref, acc, stage, sems):
    i = pl.program_id(0)
    count = count_ref[0]

    @pl.when(i == 0)
    def _():
        def clear(b, carry):
            acc[b] = jnp.zeros(acc.shape[1:], jnp.float32)
            return carry
        lax.fori_loop(0, brows, clear, 0)

    left = count - i * chunk
    turns = jnp.clip((left + unroll - 1) // unroll, 0, chunk // unroll)

    def turn(t, carry):
        for u in range(unroll):
            s = t * unroll + u
            k = i * chunk + s
            row = jnp.where(k < count, row_ref[k], brows)
            acc[row] += lax.dot_general(
                tiles_ref[s], src_ref[col_ref[k]], (((1,), (1,)), ((), ())), preferred_element_type=jnp.float32)
        return carry

    lax.fori_loop(0, turns, turn, 0)

    @pl.when(i == pl.num_programs(0) - 1)
    def _():
        size = stage.shape[1]
        total = brows // size
        def put(n):
            return pltpu.make_async_copy(stage.at[n % 2], out_ref.at[pl.ds(n * size, size)], sems.at[n % 2])
        for n in range(total):
            if n >= 2:
                put(n - 2).wait()
            def cast(b, carry):
                stage[n % 2, b] = acc[n * size + b].astype(jnp.bfloat16)
                return carry
            lax.fori_loop(0, size, cast, 0)
            put(n).start()
        for n in range(max(0, total - 2), total):
            put(n).wait()


def reduce_kernel(n_feat, parts, part_ref, weight_ref, bias_ref, out_ref,
                  own_a, own_b, got_a, got_b, y_out, y_in, z_out, z_in,
                  local_sem, a_send, a_recv, b_send, b_recv, y_send, y_recv, z_send, z_recv):
    c = lax.axis_index("col")
    f = lax.axis_index("feat")
    hi, core = c // 2, lax.rem(c, 2)
    mate = {"col": hi * 2 + (1 - core)}
    over = {"col": (1 - hi) * 2 + core}
    size = got_a.shape[2]

    barrier = pltpu.get_barrier_semaphore()
    for target in (mate, over):
        pl.semaphore_signal(barrier, inc=1, device_id=target, device_id_type=MESH)
    for d in range(1, n_feat):
        pl.semaphore_signal(barrier, inc=1, device_id={"feat": lax.rem(f + d, n_feat)}, device_id_type=MESH)
    pl.semaphore_wait(barrier, n_feat + 1)

    load_a = pltpu.make_async_copy(part_ref.at[1 - hi, core], own_a, local_sem.at[0])
    load_b = pltpu.make_async_copy(part_ref.at[hi, core], own_b, local_sem.at[1])
    load_a.start()

    def rows(t):
        return pl.ds(pl.multiple_of(t * size, size), size)

    def pair_a(t):
        return pltpu.make_async_remote_copy(
            src_ref=part_ref.at[1 - hi, 1 - core, :, rows(t), :], dst_ref=got_a.at[t],
            send_sem=a_send.at[t], recv_sem=a_recv.at[t], device_id=mate, device_id_type=MESH)

    def pair_b(t):
        return pltpu.make_async_remote_copy(
            src_ref=part_ref.at[hi, 1 - core, :, rows(t), :], dst_ref=got_b.at[t],
            send_sem=b_send.at[t], recv_sem=b_recv.at[t], device_id=mate, device_id_type=MESH)

    def swap_y(t):
        return pltpu.make_async_remote_copy(
            src_ref=y_out.at[t], dst_ref=y_in.at[t],
            send_sem=y_send.at[t], recv_sem=y_recv.at[t], device_id=over, device_id_type=MESH)

    def swap_z(t, d):
        target = lax.rem(f + d, n_feat)
        return pltpu.make_async_remote_copy(
            src_ref=z_out.at[t, target], dst_ref=z_in.at[t, d - 1],
            send_sem=z_send.at[t, d - 1], recv_sem=z_recv.at[t, d - 1],
            device_id={"feat": target}, device_id_type=MESH)

    def start_a(t, carry):
        pair_a(t).start()
        return carry

    lax.fori_loop(0, parts, start_a, 0)
    load_b.start()
    load_a.wait()
    load_b.wait()

    def turn(t, carry):
        @pl.when(t < parts)
        def _():
            pair_b(t).start()
            pair_a(t).wait_recv()
            for g in range(n_feat):
                y_out[t, g] = (own_a[g, rows(t), :].astype(jnp.float32) + got_a[t, g].astype(jnp.float32)).astype(jnp.bfloat16)
            swap_y(t).start()

        @pl.when((t >= 1) & (t < parts + 1))
        def _():
            s = t - 1
            pair_b(s).wait_recv()
            swap_y(s).wait_recv()
            for g in range(n_feat):
                z_out[s, g] = (own_b[g, rows(s), :].astype(jnp.float32) + got_b[s, g].astype(jnp.float32)
                               + y_in[s, g].astype(jnp.float32)).astype(jnp.bfloat16)
            for d in range(1, n_feat):
                swap_z(s, d).start()

        @pl.when(t >= 2)
        def _():
            s = t - 2
            total = z_out[s, f].astype(jnp.float32)
            for d in range(1, n_feat):
                swap_z(s, d).wait_recv()
                total += z_in[s, d - 1].astype(jnp.float32)
            hidden = jnp.dot(total.astype(jnp.bfloat16), weight_ref[...], preferred_element_type=jnp.float32)
            out_ref[rows(s), :] = jnp.maximum(hidden + bias_ref[...], 0.0).astype(jnp.bfloat16)
        return carry

    lax.fori_loop(0, parts + 2, turn, 0)

    def drain(t, carry):
        pair_a(t).wait_send()
        pair_b(t).wait_send()
        swap_y(t).wait_send()
        for d in range(1, n_feat):
            swap_z(t, d).wait_send()
        return carry

    lax.fori_loop(0, parts, drain, 0)


def body(n_row, n_col, n_feat, features, tiles, tile_row, tile_col, tile_count, weight, bias):
    side = tiles.shape[-1]
    slots = tiles.shape[2]
    held, width = features.shape
    fan = weight.shape[0]
    hidden = weight.shape[1]
    node_dev = held // n_feat
    brows = n_col * n_feat * node_dev // side
    blocks = held // side
    any_spec = pl.BlockSpec(memory_space=pl.ANY)
    vmem_spec = pl.BlockSpec(memory_space=pltpu.VMEM)
    dma = pltpu.SemaphoreType.DMA

    own = features.reshape(blocks, side, width).transpose(0, 2, 1)
    parts = 4
    sources = pl.pallas_call(
        functools.partial(gather_kernel, n_row, n_feat, parts),
        out_shape=jax.ShapeDtypeStruct((n_row * blocks, fan, side), jnp.bfloat16),
        in_specs=[any_spec],
        out_specs=any_spec,
        scratch_shapes=[
            dma, dma((2, n_feat - 1, parts)), dma((2, n_feat - 1, parts)),
            dma((n_row - 1, n_feat, parts)), dma((n_row - 1, n_feat, parts)),
        ],
        compiler_params=pltpu.CompilerParams(collective_id=0, has_side_effects=True),
        name="gather_sources",
    )(own)

    chunk, unroll = 32, 8
    partial_value = pl.pallas_call(
        functools.partial(tile_kernel, chunk, unroll, brows),
        out_shape=jax.ShapeDtypeStruct((brows, side, fan), jnp.bfloat16),
        grid_spec=pltpu.PrefetchScalarGridSpec(
            num_scalar_prefetch=3,
            grid=(slots // chunk,),
            in_specs=[
                pl.BlockSpec((n_row * blocks, fan, side), lambda i, n, rows, cols: (0, 0, 0), pipeline_mode=pl.Buffered(1)),
                pl.BlockSpec((chunk, side, side), lambda i, n, rows, cols: (jnp.minimum(i, (n[0] - 1) // chunk), 0, 0)),
            ],
            out_specs=any_spec,
            scratch_shapes=[
                pltpu.VMEM((brows + 1, side, fan), jnp.float32),
                pltpu.VMEM((2, 32, side, fan), jnp.bfloat16),
                dma((2,)),
            ],
        ),
        compiler_params=pltpu.CompilerParams(vmem_limit_bytes=48 * MIB),
        name="tile_products",
    )(tile_count.reshape(1), tile_row.reshape(slots), tile_col.reshape(slots), sources, tiles.reshape(slots, side, side))

    size = 128
    parts = node_dev // size
    bf = jnp.bfloat16
    return pl.pallas_call(
        functools.partial(reduce_kernel, n_feat, parts),
        out_shape=jax.ShapeDtypeStruct((node_dev, hidden), bf),
        in_specs=[any_spec, vmem_spec, vmem_spec],
        out_specs=vmem_spec,
        scratch_shapes=[
            pltpu.VMEM((n_feat, node_dev, fan), bf),
            pltpu.VMEM((n_feat, node_dev, fan), bf),
            pltpu.VMEM((parts, n_feat, size, fan), bf),
            pltpu.VMEM((parts, n_feat, size, fan), bf),
            pltpu.VMEM((parts, n_feat, size, fan), bf),
            pltpu.VMEM((parts, n_feat, size, fan), bf),
            pltpu.VMEM((parts, n_feat, size, fan), bf),
            pltpu.VMEM((parts, n_feat - 1, size, fan), bf),
            dma((2,)), dma((parts,)), dma((parts,)), dma((parts,)), dma((parts,)),
            dma((parts,)), dma((parts,)), dma((parts, n_feat - 1)), dma((parts, n_feat - 1)),
        ],
        compiler_params=pltpu.CompilerParams(collective_id=1, has_side_effects=True, vmem_limit_bytes=40 * MIB),
        name="reduce_dense",
    )(partial_value.reshape(n_col // 2, 2, n_feat, node_dev, fan), weight, bias.reshape(1, hidden))


def solution(mesh):
    placed = (
        P(("row", "col"), "feat"),
        P("row", "col", "feat", None, None),
        P("row", "col", "feat"),
        P("row", "col", "feat"),
        P("row", "col", "feat"),
        P(),
        P(),
    )
    shape = mesh.shape
    return jax.shard_map(
        functools.partial(body, shape["row"], shape["col"], shape["feat"]),
        mesh=mesh, in_specs=placed, out_specs=P(("row", "col", "feat"), None), check_vma=False
    )
```

```python
import functools

import jax
import jax.numpy as jnp
from jax import lax
from jax.experimental import pallas as pl
from jax.experimental.pallas import tpu as pltpu
from jax.sharding import PartitionSpec as P

MESH = pl.DeviceIdType.MESH
MIB = 1 << 20


def gather_kernel(n_row, n_feat, parts, own_ref, out_ref, local_sem, z_send, z_recv, x_send, x_recv):
    r = lax.axis_index("row")
    f = lax.axis_index("feat")
    blocks, width = own_ref.shape[0], own_ref.shape[1]
    step = blocks // parts

    barrier = pltpu.get_barrier_semaphore()
    for p in range(1, n_row):
        pl.semaphore_signal(barrier, inc=1, device_id={"row": lax.rem(r + p, n_row)}, device_id_type=MESH)

    @pl.when(f > 0)
    def _():
        pl.semaphore_signal(barrier, inc=1, device_id={"feat": f - 1}, device_id_type=MESH)

    @pl.when(f < n_feat - 1)
    def _():
        pl.semaphore_signal(barrier, inc=1, device_id={"feat": f + 1}, device_id_type=MESH)

    ends = jnp.where(f > 0, 1, 0) + jnp.where(f < n_feat - 1, 1, 0)
    pl.semaphore_wait(barrier, n_row - 1 + ends)

    def region(row, feat, c):
        return out_ref.at[pl.ds(row * blocks + c * step, step), pl.ds(pl.multiple_of(feat * width, width), width), :]

    def own(c):
        return own_ref.at[pl.ds(c * step, step)]

    def along(way, hop, c, origin, src=None):
        target = f + 1 if way == 0 else f - 1
        place = region(r, origin, c)
        return pltpu.make_async_remote_copy(
            src_ref=place if src is None else src, dst_ref=place,
            send_sem=z_send.at[way, hop, c], recv_sem=z_recv.at[way, hop, c],
            device_id={"feat": target}, device_id_type=MESH)

    def across(p, origin, c, src=None):
        place = region(r, origin, c)
        return pltpu.make_async_remote_copy(
            src_ref=place if src is None else src, dst_ref=place,
            send_sem=x_send.at[p - 1, origin, c], recv_sem=x_recv.at[p - 1, origin, c],
            device_id={"row": lax.rem(r + p, n_row)}, device_id_type=MESH)

    for c in range(parts):
        @pl.when(f < n_feat - 1)
        def _():
            along(0, 0, c, f, own(c)).start()

        @pl.when(f > 0)
        def _():
            along(1, 0, c, f, own(c)).start()

        for p in range(1, n_row):
            across(p, f, c, own(c)).start()
    local = pltpu.make_async_copy(own_ref, out_ref.at[pl.ds(r * blocks, blocks), pl.ds(pl.multiple_of(f * width, width), width), :], local_sem)
    local.start()

    for hop in range(1, n_feat):
        for c in range(parts):
            @pl.when(f - hop >= 0)
            def _():
                origin = f - hop
                along(0, hop - 1, c, origin).wait_recv()
                if hop < n_feat - 1:
                    @pl.when(f < n_feat - 1)
                    def _():
                        along(0, hop, c, origin).start()
                for p in range(1, n_row):
                    across(p, origin, c).start()

            @pl.when(f + hop < n_feat)
            def _():
                origin = f + hop
                along(1, hop - 1, c, origin).wait_recv()
                if hop < n_feat - 1:
                    @pl.when(f > 0)
                    def _():
                        along(1, hop, c, origin).start()
                for p in range(1, n_row):
                    across(p, origin, c).start()

    for origin in range(n_feat):
        for c in range(parts):
            for p in range(1, n_row):
                across(p, origin, c).wait()
    for hop in range(n_feat - 1):
        for c in range(parts):
            @pl.when((f < n_feat - 1) & (f - hop >= 0))
            def _():
                along(0, hop, c, f - hop).wait_send()

            @pl.when((f > 0) & (f + hop < n_feat))
            def _():
                along(1, hop, c, f + hop).wait_send()
    local.wait()


def tile_kernel(chunk, unroll, brows, count_ref, row_ref, col_ref, src_ref, tiles_ref, out_ref, acc, stage, sems):
    i = pl.program_id(0)
    count = count_ref[0]

    @pl.when(i == 0)
    def _():
        def clear(b, carry):
            acc[b] = jnp.zeros(acc.shape[1:], jnp.float32)
            return carry
        lax.fori_loop(0, brows, clear, 0)

    left = count - i * chunk
    turns = jnp.clip((left + unroll - 1) // unroll, 0, chunk // unroll)

    def turn(t, carry):
        for u in range(unroll):
            s = t * unroll + u
            k = i * chunk + s
            row = jnp.where(k < count, row_ref[k], brows)
            acc[row] += lax.dot_general(
                tiles_ref[s], src_ref[col_ref[k]], (((1,), (1,)), ((), ())), preferred_element_type=jnp.float32)
        return carry

    lax.fori_loop(0, turns, turn, 0)

    @pl.when(i == pl.num_programs(0) - 1)
    def _():
        size = stage.shape[1]
        total = brows // size
        def put(n):
            return pltpu.make_async_copy(stage.at[n % 2], out_ref.at[pl.ds(n * size, size)], sems.at[n % 2])
        for n in range(total):
            if n >= 2:
                put(n - 2).wait()
            def cast(b, carry):
                stage[n % 2, b] = acc[n * size + b].astype(jnp.bfloat16)
                return carry
            lax.fori_loop(0, size, cast, 0)
            put(n).start()
        for n in range(max(0, total - 2), total):
            put(n).wait()


def reduce_kernel(n_feat, parts, part_ref, weight_ref, bias_ref, out_ref,
                  own_a, own_b, got_a, got_b, y_out, y_in, z_out, z_in,
                  local_sem, a_send, a_recv, b_send, b_recv, y_send, y_recv, z_send, z_recv):
    c = lax.axis_index("col")
    f = lax.axis_index("feat")
    hi, core = c // 2, lax.rem(c, 2)
    mate = {"col": hi * 2 + (1 - core)}
    over = {"col": (1 - hi) * 2 + core}
    size = got_a.shape[2]

    barrier = pltpu.get_barrier_semaphore()
    for target in (mate, over):
        pl.semaphore_signal(barrier, inc=1, device_id=target, device_id_type=MESH)
    for d in range(1, n_feat):
        pl.semaphore_signal(barrier, inc=1, device_id={"feat": lax.rem(f + d, n_feat)}, device_id_type=MESH)
    pl.semaphore_wait(barrier, n_feat + 1)

    load_a = pltpu.make_async_copy(part_ref.at[1 - hi, core], own_a, local_sem.at[0])
    load_b = pltpu.make_async_copy(part_ref.at[hi, core], own_b, local_sem.at[1])
    load_a.start()

    def rows(t):
        return pl.ds(pl.multiple_of(t * size, size), size)

    def pair_a(t):
        return pltpu.make_async_remote_copy(
            src_ref=part_ref.at[1 - hi, 1 - core, :, rows(t), :], dst_ref=got_a.at[t],
            send_sem=a_send.at[t], recv_sem=a_recv.at[t], device_id=mate, device_id_type=MESH)

    def pair_b(t):
        return pltpu.make_async_remote_copy(
            src_ref=part_ref.at[hi, 1 - core, :, rows(t), :], dst_ref=got_b.at[t],
            send_sem=b_send.at[t], recv_sem=b_recv.at[t], device_id=mate, device_id_type=MESH)

    def swap_y(t):
        return pltpu.make_async_remote_copy(
            src_ref=y_out.at[t], dst_ref=y_in.at[t],
            send_sem=y_send.at[t], recv_sem=y_recv.at[t], device_id=over, device_id_type=MESH)

    def swap_z(t, d):
        target = lax.rem(f + d, n_feat)
        return pltpu.make_async_remote_copy(
            src_ref=z_out.at[t, target], dst_ref=z_in.at[t, d - 1],
            send_sem=z_send.at[t, d - 1], recv_sem=z_recv.at[t, d - 1],
            device_id={"feat": target}, device_id_type=MESH)

    def start_a(t, carry):
        pair_a(t).start()
        return carry

    lax.fori_loop(0, parts, start_a, 0)
    load_b.start()
    load_a.wait()
    load_b.wait()

    def turn(t, carry):
        @pl.when(t < parts)
        def _():
            pair_b(t).start()
            pair_a(t).wait_recv()
            for g in range(n_feat):
                y_out[t, g] = (own_a[g, rows(t), :].astype(jnp.float32) + got_a[t, g].astype(jnp.float32)).astype(jnp.bfloat16)
            swap_y(t).start()

        @pl.when((t >= 1) & (t < parts + 1))
        def _():
            s = t - 1
            pair_b(s).wait_recv()
            swap_y(s).wait_recv()
            for g in range(n_feat):
                z_out[s, g] = (own_b[g, rows(s), :].astype(jnp.float32) + got_b[s, g].astype(jnp.float32)
                               + y_in[s, g].astype(jnp.float32)).astype(jnp.bfloat16)
            for d in range(1, n_feat):
                swap_z(s, d).start()

        @pl.when(t >= 2)
        def _():
            s = t - 2
            total = z_out[s, f].astype(jnp.float32)
            for d in range(1, n_feat):
                swap_z(s, d).wait_recv()
                total += z_in[s, d - 1].astype(jnp.float32)
            hidden = jnp.dot(total.astype(jnp.bfloat16), weight_ref[...], preferred_element_type=jnp.float32)
            out_ref[rows(s), :] = jnp.maximum(hidden + bias_ref[...], 0.0).astype(jnp.bfloat16)
        return carry

    lax.fori_loop(0, parts + 2, turn, 0)

    def drain(t, carry):
        pair_a(t).wait_send()
        pair_b(t).wait_send()
        swap_y(t).wait_send()
        for d in range(1, n_feat):
            swap_z(t, d).wait_send()
        return carry

    lax.fori_loop(0, parts, drain, 0)


def body(n_row, n_col, n_feat, features, tiles, tile_row, tile_col, tile_count, weight, bias):
    side = tiles.shape[-1]
    slots = tiles.shape[2]
    held, width = features.shape
    fan = weight.shape[0]
    hidden = weight.shape[1]
    node_dev = held // n_feat
    brows = n_col * n_feat * node_dev // side
    blocks = held // side
    any_spec = pl.BlockSpec(memory_space=pl.ANY)
    vmem_spec = pl.BlockSpec(memory_space=pltpu.VMEM)
    dma = pltpu.SemaphoreType.DMA

    own = features.reshape(blocks, side, width).transpose(0, 2, 1)
    parts = 8
    sources = pl.pallas_call(
        functools.partial(gather_kernel, n_row, n_feat, parts),
        out_shape=jax.ShapeDtypeStruct((n_row * blocks, fan, side), jnp.bfloat16),
        in_specs=[any_spec],
        out_specs=any_spec,
        scratch_shapes=[
            dma, dma((2, n_feat - 1, parts)), dma((2, n_feat - 1, parts)),
            dma((n_row - 1, n_feat, parts)), dma((n_row - 1, n_feat, parts)),
        ],
        compiler_params=pltpu.CompilerParams(collective_id=0, has_side_effects=True),
        name="gather_sources",
    )(own)

    chunk, unroll = 32, 8
    partial_value = pl.pallas_call(
        functools.partial(tile_kernel, chunk, unroll, brows),
        out_shape=jax.ShapeDtypeStruct((brows, side, fan), jnp.bfloat16),
        grid_spec=pltpu.PrefetchScalarGridSpec(
            num_scalar_prefetch=3,
            grid=(slots // chunk,),
            in_specs=[
                pl.BlockSpec((n_row * blocks, fan, side), lambda i, n, rows, cols: (0, 0, 0), pipeline_mode=pl.Buffered(1)),
                pl.BlockSpec((chunk, side, side), lambda i, n, rows, cols: (jnp.minimum(i, (n[0] - 1) // chunk), 0, 0)),
            ],
            out_specs=any_spec,
            scratch_shapes=[
                pltpu.VMEM((brows + 1, side, fan), jnp.float32),
                pltpu.VMEM((2, 32, side, fan), jnp.bfloat16),
                dma((2,)),
            ],
        ),
        compiler_params=pltpu.CompilerParams(vmem_limit_bytes=60 * MIB),
        name="tile_products",
    )(tile_count.reshape(1), tile_row.reshape(slots), tile_col.reshape(slots), sources, tiles.reshape(slots, side, side))

    size = 128
    parts = node_dev // size
    bf = jnp.bfloat16
    return pl.pallas_call(
        functools.partial(reduce_kernel, n_feat, parts),
        out_shape=jax.ShapeDtypeStruct((node_dev, hidden), bf),
        in_specs=[any_spec, vmem_spec, vmem_spec],
        out_specs=vmem_spec,
        scratch_shapes=[
            pltpu.VMEM((n_feat, node_dev, fan), bf),
            pltpu.VMEM((n_feat, node_dev, fan), bf),
            pltpu.VMEM((parts, n_feat, size, fan), bf),
            pltpu.VMEM((parts, n_feat, size, fan), bf),
            pltpu.VMEM((parts, n_feat, size, fan), bf),
            pltpu.VMEM((parts, n_feat, size, fan), bf),
            pltpu.VMEM((parts, n_feat, size, fan), bf),
            pltpu.VMEM((parts, n_feat - 1, size, fan), bf),
            dma((2,)), dma((parts,)), dma((parts,)), dma((parts,)), dma((parts,)),
            dma((parts,)), dma((parts,)), dma((parts, n_feat - 1)), dma((parts, n_feat - 1)),
        ],
        compiler_params=pltpu.CompilerParams(collective_id=1, has_side_effects=True, vmem_limit_bytes=60 * MIB),
        name="reduce_dense",
    )(partial_value.reshape(n_col // 2, 2, n_feat, node_dev, fan), weight, bias.reshape(1, hidden))


def solution(mesh):
    placed = (
        P(("row", "col"), "feat"),
        P("row", "col", "feat", None, None),
        P("row", "col", "feat"),
        P("row", "col", "feat"),
        P("row", "col", "feat"),
        P(),
        P(),
    )
    shape = mesh.shape
    return jax.shard_map(
        functools.partial(body, shape["row"], shape["col"], shape["feat"]),
        mesh=mesh, in_specs=placed, out_specs=P(("row", "col", "feat"), None), check_vma=False
    )
```

```python
import functools

import jax
import jax.numpy as jnp
from jax import lax
from jax.experimental import pallas as pl
from jax.experimental.pallas import tpu as pltpu
from jax.sharding import PartitionSpec as P

MESH = pl.DeviceIdType.MESH
MIB = 1 << 20


def gather_kernel(n_row, n_feat, parts, own_ref, out_ref, local_sem, z_send, z_recv, x_send, x_recv):
    r = lax.axis_index("row")
    f = lax.axis_index("feat")
    blocks, width = own_ref.shape[0], own_ref.shape[1]
    step = blocks // parts

    barrier = pltpu.get_barrier_semaphore()
    for p in range(1, n_row):
        pl.semaphore_signal(barrier, inc=1, device_id={"row": lax.rem(r + p, n_row)}, device_id_type=MESH)

    @pl.when(f > 0)
    def _():
        pl.semaphore_signal(barrier, inc=1, device_id={"feat": f - 1}, device_id_type=MESH)

    @pl.when(f < n_feat - 1)
    def _():
        pl.semaphore_signal(barrier, inc=1, device_id={"feat": f + 1}, device_id_type=MESH)

    ends = jnp.where(f > 0, 1, 0) + jnp.where(f < n_feat - 1, 1, 0)
    pl.semaphore_wait(barrier, n_row - 1 + ends)

    def region(row, feat, c):
        return out_ref.at[pl.ds(row * blocks + c * step, step), pl.ds(pl.multiple_of(feat * width, width), width), :]

    def own(c):
        return own_ref.at[pl.ds(c * step, step)]

    def along(way, hop, c, origin, src=None):
        target = f + 1 if way == 0 else f - 1
        place = region(r, origin, c)
        return pltpu.make_async_remote_copy(
            src_ref=place if src is None else src, dst_ref=place,
            send_sem=z_send.at[way, hop, c], recv_sem=z_recv.at[way, hop, c],
            device_id={"feat": target}, device_id_type=MESH)

    def across(p, origin, c, src=None):
        place = region(r, origin, c)
        return pltpu.make_async_remote_copy(
            src_ref=place if src is None else src, dst_ref=place,
            send_sem=x_send.at[p - 1, origin, c], recv_sem=x_recv.at[p - 1, origin, c],
            device_id={"row": lax.rem(r + p, n_row)}, device_id_type=MESH)

    for c in range(parts):
        @pl.when(f < n_feat - 1)
        def _():
            along(0, 0, c, f, own(c)).start()

        @pl.when(f > 0)
        def _():
            along(1, 0, c, f, own(c)).start()

        for p in range(1, n_row):
            across(p, f, c, own(c)).start()
    local = pltpu.make_async_copy(own_ref, out_ref.at[pl.ds(r * blocks, blocks), pl.ds(pl.multiple_of(f * width, width), width), :], local_sem)
    local.start()

    for hop in range(1, n_feat):
        for c in range(parts):
            @pl.when(f - hop >= 0)
            def _():
                origin = f - hop
                along(0, hop - 1, c, origin).wait_recv()
                if hop < n_feat - 1:
                    @pl.when(f < n_feat - 1)
                    def _():
                        along(0, hop, c, origin).start()
                for p in range(1, n_row):
                    across(p, origin, c).start()

            @pl.when(f + hop < n_feat)
            def _():
                origin = f + hop
                along(1, hop - 1, c, origin).wait_recv()
                if hop < n_feat - 1:
                    @pl.when(f > 0)
                    def _():
                        along(1, hop, c, origin).start()
                for p in range(1, n_row):
                    across(p, origin, c).start()

    for origin in range(n_feat):
        for c in range(parts):
            for p in range(1, n_row):
                across(p, origin, c).wait()
    for hop in range(n_feat - 1):
        for c in range(parts):
            @pl.when((f < n_feat - 1) & (f - hop >= 0))
            def _():
                along(0, hop, c, f - hop).wait_send()

            @pl.when((f > 0) & (f + hop < n_feat))
            def _():
                along(1, hop, c, f + hop).wait_send()
    local.wait()


def tile_kernel(chunk, unroll, brows, count_ref, row_ref, col_ref, src_ref, tiles_ref, out_ref, acc, stage, sems):
    i = pl.program_id(0)
    count = count_ref[0]

    @pl.when(i == 0)
    def _():
        def clear(b, carry):
            acc[b] = jnp.zeros(acc.shape[1:], jnp.float32)
            return carry
        lax.fori_loop(0, brows, clear, 0)

    left = count - i * chunk
    turns = jnp.clip((left + unroll - 1) // unroll, 0, chunk // unroll)

    def turn(t, carry):
        for u in range(unroll):
            s = t * unroll + u
            k = i * chunk + s
            row = jnp.where(k < count, row_ref[k], brows)
            acc[row] += lax.dot_general(
                tiles_ref[s], src_ref[col_ref[k]], (((1,), (1,)), ((), ())), preferred_element_type=jnp.float32)
        return carry

    lax.fori_loop(0, turns, turn, 0)

    @pl.when(i == pl.num_programs(0) - 1)
    def _():
        size = stage.shape[1]
        total = brows // size
        def put(n):
            return pltpu.make_async_copy(stage.at[n % 2], out_ref.at[pl.ds(n * size, size)], sems.at[n % 2])
        for n in range(total):
            if n >= 2:
                put(n - 2).wait()
            def cast(b, carry):
                stage[n % 2, b] = acc[n * size + b].astype(jnp.bfloat16)
                return carry
            lax.fori_loop(0, size, cast, 0)
            put(n).start()
        for n in range(max(0, total - 2), total):
            put(n).wait()


def reduce_kernel(n_feat, parts, part_ref, weight_ref, bias_ref, out_ref,
                  own_a, own_b, got_a, got_b, y_out, y_in, z_out, z_in,
                  local_sem, a_send, a_recv, b_send, b_recv, y_send, y_recv, z_send, z_recv):
    c = lax.axis_index("col")
    f = lax.axis_index("feat")
    hi, core = c // 2, lax.rem(c, 2)
    mate = {"col": hi * 2 + (1 - core)}
    over = {"col": (1 - hi) * 2 + core}
    size = got_a.shape[2]

    barrier = pltpu.get_barrier_semaphore()
    for target in (mate, over):
        pl.semaphore_signal(barrier, inc=1, device_id=target, device_id_type=MESH)
    for d in range(1, n_feat):
        pl.semaphore_signal(barrier, inc=1, device_id={"feat": lax.rem(f + d, n_feat)}, device_id_type=MESH)
    pl.semaphore_wait(barrier, n_feat + 1)

    load_a = pltpu.make_async_copy(part_ref.at[1 - hi, core], own_a, local_sem.at[0])
    load_b = pltpu.make_async_copy(part_ref.at[hi, core], own_b, local_sem.at[1])
    load_a.start()

    def rows(t):
        return pl.ds(pl.multiple_of(t * size, size), size)

    def pair_a(t):
        return pltpu.make_async_remote_copy(
            src_ref=part_ref.at[1 - hi, 1 - core, :, rows(t), :], dst_ref=got_a.at[t],
            send_sem=a_send.at[t], recv_sem=a_recv.at[t], device_id=mate, device_id_type=MESH)

    def pair_b(t):
        return pltpu.make_async_remote_copy(
            src_ref=part_ref.at[hi, 1 - core, :, rows(t), :], dst_ref=got_b.at[t],
            send_sem=b_send.at[t], recv_sem=b_recv.at[t], device_id=mate, device_id_type=MESH)

    def swap_y(t):
        return pltpu.make_async_remote_copy(
            src_ref=y_out.at[t], dst_ref=y_in.at[t],
            send_sem=y_send.at[t], recv_sem=y_recv.at[t], device_id=over, device_id_type=MESH)

    def swap_z(t, d):
        target = lax.rem(f + d, n_feat)
        return pltpu.make_async_remote_copy(
            src_ref=z_out.at[t, target], dst_ref=z_in.at[t, d - 1],
            send_sem=z_send.at[t, d - 1], recv_sem=z_recv.at[t, d - 1],
            device_id={"feat": target}, device_id_type=MESH)

    def start_a(t, carry):
        pair_a(t).start()
        return carry

    lax.fori_loop(0, parts, start_a, 0)
    load_b.start()
    load_a.wait()
    load_b.wait()

    def turn(t, carry):
        @pl.when(t < parts)
        def _():
            pair_b(t).start()
            pair_a(t).wait_recv()
            for g in range(n_feat):
                y_out[t, g] = (own_a[g, rows(t), :].astype(jnp.float32) + got_a[t, g].astype(jnp.float32)).astype(jnp.bfloat16)
            swap_y(t).start()

        @pl.when((t >= 1) & (t < parts + 1))
        def _():
            s = t - 1
            pair_b(s).wait_recv()
            swap_y(s).wait_recv()
            for g in range(n_feat):
                z_out[s, g] = (own_b[g, rows(s), :].astype(jnp.float32) + got_b[s, g].astype(jnp.float32)
                               + y_in[s, g].astype(jnp.float32)).astype(jnp.bfloat16)
            for d in range(1, n_feat):
                swap_z(s, d).start()

        @pl.when(t >= 2)
        def _():
            s = t - 2
            total = z_out[s, f].astype(jnp.float32)
            for d in range(1, n_feat):
                swap_z(s, d).wait_recv()
                total += z_in[s, d - 1].astype(jnp.float32)
            hidden = jnp.dot(total.astype(jnp.bfloat16), weight_ref[...], preferred_element_type=jnp.float32)
            out_ref[rows(s), :] = jnp.maximum(hidden + bias_ref[...], 0.0).astype(jnp.bfloat16)
        return carry

    lax.fori_loop(0, parts + 2, turn, 0)

    def drain(t, carry):
        pair_a(t).wait_send()
        pair_b(t).wait_send()
        swap_y(t).wait_send()
        for d in range(1, n_feat):
            swap_z(t, d).wait_send()
        return carry

    lax.fori_loop(0, parts, drain, 0)


def body(n_row, n_col, n_feat, features, tiles, tile_row, tile_col, tile_count, weight, bias):
    side = tiles.shape[-1]
    slots = tiles.shape[2]
    held, width = features.shape
    fan = weight.shape[0]
    hidden = weight.shape[1]
    node_dev = held // n_feat
    brows = n_col * n_feat * node_dev // side
    blocks = held // side
    any_spec = pl.BlockSpec(memory_space=pl.ANY)
    vmem_spec = pl.BlockSpec(memory_space=pltpu.VMEM)
    dma = pltpu.SemaphoreType.DMA

    own = features.reshape(blocks, side, width).transpose(0, 2, 1)
    parts = 4
    sources = pl.pallas_call(
        functools.partial(gather_kernel, n_row, n_feat, parts),
        out_shape=jax.ShapeDtypeStruct((n_row * blocks, fan, side), jnp.bfloat16),
        in_specs=[any_spec],
        out_specs=any_spec,
        scratch_shapes=[
            dma, dma((2, n_feat - 1, parts)), dma((2, n_feat - 1, parts)),
            dma((n_row - 1, n_feat, parts)), dma((n_row - 1, n_feat, parts)),
        ],
        compiler_params=pltpu.CompilerParams(collective_id=0, has_side_effects=True),
        name="gather_sources",
    )(own)

    chunk, unroll = 32, 8
    partial_value = pl.pallas_call(
        functools.partial(tile_kernel, chunk, unroll, brows),
        out_shape=jax.ShapeDtypeStruct((brows, side, fan), jnp.bfloat16),
        grid_spec=pltpu.PrefetchScalarGridSpec(
            num_scalar_prefetch=3,
            grid=(slots // chunk,),
            in_specs=[
                pl.BlockSpec((n_row * blocks, fan, side), lambda i, n, rows, cols: (0, 0, 0), pipeline_mode=pl.Buffered(1)),
                pl.BlockSpec((chunk, side, side), lambda i, n, rows, cols: (jnp.minimum(i, (n[0] - 1) // chunk), 0, 0)),
            ],
            out_specs=any_spec,
            scratch_shapes=[
                pltpu.VMEM((brows + 1, side, fan), jnp.float32),
                pltpu.VMEM((2, 32, side, fan), jnp.bfloat16),
                dma((2,)),
            ],
        ),
        compiler_params=pltpu.CompilerParams(vmem_limit_bytes=60 * MIB),
        name="tile_products",
    )(tile_count.reshape(1), tile_row.reshape(slots), tile_col.reshape(slots), sources, tiles.reshape(slots, side, side))

    size = 128
    parts = node_dev // size
    bf = jnp.bfloat16
    return pl.pallas_call(
        functools.partial(reduce_kernel, n_feat, parts),
        out_shape=jax.ShapeDtypeStruct((node_dev, hidden), bf),
        in_specs=[any_spec, vmem_spec, vmem_spec],
        out_specs=vmem_spec,
        scratch_shapes=[
            pltpu.VMEM((n_feat, node_dev, fan), bf),
            pltpu.VMEM((n_feat, node_dev, fan), bf),
            pltpu.VMEM((parts, n_feat, size, fan), bf),
            pltpu.VMEM((parts, n_feat, size, fan), bf),
            pltpu.VMEM((parts, n_feat, size, fan), bf),
            pltpu.VMEM((parts, n_feat, size, fan), bf),
            pltpu.VMEM((parts, n_feat, size, fan), bf),
            pltpu.VMEM((parts, n_feat - 1, size, fan), bf),
            dma((2,)), dma((parts,)), dma((parts,)), dma((parts,)), dma((parts,)),
            dma((parts,)), dma((parts,)), dma((parts, n_feat - 1)), dma((parts, n_feat - 1)),
        ],
        compiler_params=pltpu.CompilerParams(collective_id=1, has_side_effects=True, vmem_limit_bytes=40 * MIB),
        name="reduce_dense",
    )(partial_value.reshape(n_col // 2, 2, n_feat, node_dev, fan), weight, bias.reshape(1, hidden))


def solution(mesh):
    placed = (
        P(("row", "col"), "feat"),
        P("row", "col", "feat", None, None),
        P("row", "col", "feat"),
        P("row", "col", "feat"),
        P("row", "col", "feat"),
        P(),
        P(),
    )
    shape = mesh.shape
    return jax.shard_map(
        functools.partial(body, shape["row"], shape["col"], shape["feat"]),
        mesh=mesh, in_specs=placed, out_specs=P(("row", "col", "feat"), None), check_vma=False
    )
```

```python
import functools

import jax
import jax.numpy as jnp
from jax import lax
from jax.experimental import pallas as pl
from jax.experimental.pallas import tpu as pltpu
from jax.sharding import PartitionSpec as P

MESH = pl.DeviceIdType.MESH
MIB = 1 << 20


def gather_kernel(n_row, n_feat, parts, own_ref, out_ref, local_sem, z_send, z_recv, x_send, x_recv):
    r = lax.axis_index("row")
    f = lax.axis_index("feat")
    blocks, width = own_ref.shape[0], own_ref.shape[1]
    step = blocks // parts

    barrier = pltpu.get_barrier_semaphore()
    for p in range(1, n_row):
        pl.semaphore_signal(barrier, inc=1, device_id={"row": lax.rem(r + p, n_row)}, device_id_type=MESH)

    @pl.when(f > 0)
    def _():
        pl.semaphore_signal(barrier, inc=1, device_id={"feat": f - 1}, device_id_type=MESH)

    @pl.when(f < n_feat - 1)
    def _():
        pl.semaphore_signal(barrier, inc=1, device_id={"feat": f + 1}, device_id_type=MESH)

    ends = jnp.where(f > 0, 1, 0) + jnp.where(f < n_feat - 1, 1, 0)
    pl.semaphore_wait(barrier, n_row - 1 + ends)

    def region(row, feat, c):
        return out_ref.at[pl.ds(row * blocks + c * step, step), pl.ds(pl.multiple_of(feat * width, width), width), :]

    def own(c):
        return own_ref.at[pl.ds(c * step, step)]

    def along(way, hop, c, origin, src=None):
        target = f + 1 if way == 0 else f - 1
        place = region(r, origin, c)
        return pltpu.make_async_remote_copy(
            src_ref=place if src is None else src, dst_ref=place,
            send_sem=z_send.at[way, hop, c], recv_sem=z_recv.at[way, hop, c],
            device_id={"feat": target}, device_id_type=MESH)

    def across(p, origin, c, src=None):
        place = region(r, origin, c)
        return pltpu.make_async_remote_copy(
            src_ref=place if src is None else src, dst_ref=place,
            send_sem=x_send.at[p - 1, origin, c], recv_sem=x_recv.at[p - 1, origin, c],
            device_id={"row": lax.rem(r + p, n_row)}, device_id_type=MESH)

    for c in range(parts):
        @pl.when(f < n_feat - 1)
        def _():
            along(0, 0, c, f, own(c)).start()

        @pl.when(f > 0)
        def _():
            along(1, 0, c, f, own(c)).start()

        for p in range(1, n_row):
            across(p, f, c, own(c)).start()
    local = pltpu.make_async_copy(own_ref, out_ref.at[pl.ds(r * blocks, blocks), pl.ds(pl.multiple_of(f * width, width), width), :], local_sem)
    local.start()

    for hop in range(1, n_feat):
        for c in range(parts):
            @pl.when(f - hop >= 0)
            def _():
                origin = f - hop
                along(0, hop - 1, c, origin).wait_recv()
                if hop < n_feat - 1:
                    @pl.when(f < n_feat - 1)
                    def _():
                        along(0, hop, c, origin).start()
                for p in range(1, n_row):
                    across(p, origin, c).start()

            @pl.when(f + hop < n_feat)
            def _():
                origin = f + hop
                along(1, hop - 1, c, origin).wait_recv()
                if hop < n_feat - 1:
                    @pl.when(f > 0)
                    def _():
                        along(1, hop, c, origin).start()
                for p in range(1, n_row):
                    across(p, origin, c).start()

    for origin in range(n_feat):
        for c in range(parts):
            for p in range(1, n_row):
                across(p, origin, c).wait()
    for hop in range(n_feat - 1):
        for c in range(parts):
            @pl.when((f < n_feat - 1) & (f - hop >= 0))
            def _():
                along(0, hop, c, f - hop).wait_send()

            @pl.when((f > 0) & (f + hop < n_feat))
            def _():
                along(1, hop, c, f + hop).wait_send()
    local.wait()


def tile_kernel(chunk, unroll, brows, count_ref, row_ref, col_ref, src_ref, tiles_ref, out_ref, acc, stage, sems):
    i = pl.program_id(0)
    count = count_ref[0]

    @pl.when(i == 0)
    def _():
        def clear(b, carry):
            acc[b] = jnp.zeros(acc.shape[1:], jnp.float32)
            return carry
        lax.fori_loop(0, brows, clear, 0, unroll=4)

    left = count - i * chunk
    turns = jnp.clip((left + unroll - 1) // unroll, 0, chunk // unroll)

    def turn(t, carry):
        for u in range(unroll):
            s = t * unroll + u
            k = i * chunk + s
            row = jnp.where(k < count, row_ref[k], brows)
            acc[row] += lax.dot_general(
                tiles_ref[s], src_ref[col_ref[k]], (((1,), (1,)), ((), ())), preferred_element_type=jnp.float32)
        return carry

    lax.fori_loop(0, turns, turn, 0)

    @pl.when(i == pl.num_programs(0) - 1)
    def _():
        size = stage.shape[1]
        total = brows // size
        def put(n):
            return pltpu.make_async_copy(stage.at[n % 2], out_ref.at[pl.ds(n * size, size)], sems.at[n % 2])
        for n in range(total):
            if n >= 2:
                put(n - 2).wait()
            def cast(b, carry):
                stage[n % 2, b] = acc[n * size + b].astype(jnp.bfloat16)
                return carry
            lax.fori_loop(0, size, cast, 0, unroll=4)
            put(n).start()
        for n in range(max(0, total - 2), total):
            put(n).wait()


def reduce_kernel(n_feat, parts, part_ref, weight_ref, bias_ref, out_ref,
                  own_a, own_b, got_a, got_b, y_out, y_in, z_out, z_in,
                  local_sem, a_send, a_recv, b_send, b_recv, y_send, y_recv, z_send, z_recv):
    c = lax.axis_index("col")
    f = lax.axis_index("feat")
    hi, core = c // 2, lax.rem(c, 2)
    mate = {"col": hi * 2 + (1 - core)}
    over = {"col": (1 - hi) * 2 + core}
    size = got_a.shape[2]

    barrier = pltpu.get_barrier_semaphore()
    for target in (mate, over):
        pl.semaphore_signal(barrier, inc=1, device_id=target, device_id_type=MESH)
    for d in range(1, n_feat):
        pl.semaphore_signal(barrier, inc=1, device_id={"feat": lax.rem(f + d, n_feat)}, device_id_type=MESH)
    pl.semaphore_wait(barrier, n_feat + 1)

    load_a = pltpu.make_async_copy(part_ref.at[1 - hi, core], own_a, local_sem.at[0])
    load_b = pltpu.make_async_copy(part_ref.at[hi, core], own_b, local_sem.at[1])
    load_a.start()

    def rows(t):
        return pl.ds(pl.multiple_of(t * size, size), size)

    def pair_a(t):
        return pltpu.make_async_remote_copy(
            src_ref=part_ref.at[1 - hi, 1 - core, :, rows(t), :], dst_ref=got_a.at[t],
            send_sem=a_send.at[t], recv_sem=a_recv.at[t], device_id=mate, device_id_type=MESH)

    def pair_b(t):
        return pltpu.make_async_remote_copy(
            src_ref=part_ref.at[hi, 1 - core, :, rows(t), :], dst_ref=got_b.at[t],
            send_sem=b_send.at[t], recv_sem=b_recv.at[t], device_id=mate, device_id_type=MESH)

    def swap_y(t):
        return pltpu.make_async_remote_copy(
            src_ref=y_out.at[t], dst_ref=y_in.at[t],
            send_sem=y_send.at[t], recv_sem=y_recv.at[t], device_id=over, device_id_type=MESH)

    def swap_z(t, d):
        target = lax.rem(f + d, n_feat)
        return pltpu.make_async_remote_copy(
            src_ref=z_out.at[t, target], dst_ref=z_in.at[t, d - 1],
            send_sem=z_send.at[t, d - 1], recv_sem=z_recv.at[t, d - 1],
            device_id={"feat": target}, device_id_type=MESH)

    def start_a(t, carry):
        pair_a(t).start()
        return carry

    lax.fori_loop(0, parts, start_a, 0)
    load_b.start()
    load_a.wait()
    load_b.wait()

    def turn(t, carry):
        @pl.when(t < parts)
        def _():
            pair_b(t).start()
            pair_a(t).wait_recv()
            for g in range(n_feat):
                y_out[t, g] = (own_a[g, rows(t), :].astype(jnp.float32) + got_a[t, g].astype(jnp.float32)).astype(jnp.bfloat16)
            swap_y(t).start()

        @pl.when((t >= 1) & (t < parts + 1))
        def _():
            s = t - 1
            pair_b(s).wait_recv()
            swap_y(s).wait_recv()
            for g in range(n_feat):
                z_out[s, g] = (own_b[g, rows(s), :].astype(jnp.float32) + got_b[s, g].astype(jnp.float32)
                               + y_in[s, g].astype(jnp.float32)).astype(jnp.bfloat16)
            for d in range(1, n_feat):
                swap_z(s, d).start()

        @pl.when(t >= 2)
        def _():
            s = t - 2
            total = z_out[s, f].astype(jnp.float32)
            for d in range(1, n_feat):
                swap_z(s, d).wait_recv()
                total += z_in[s, d - 1].astype(jnp.float32)
            hidden = jnp.dot(total.astype(jnp.bfloat16), weight_ref[...], preferred_element_type=jnp.float32)
            out_ref[rows(s), :] = jnp.maximum(hidden + bias_ref[...], 0.0).astype(jnp.bfloat16)
        return carry

    lax.fori_loop(0, parts + 2, turn, 0)

    def drain(t, carry):
        pair_a(t).wait_send()
        pair_b(t).wait_send()
        swap_y(t).wait_send()
        for d in range(1, n_feat):
            swap_z(t, d).wait_send()
        return carry

    lax.fori_loop(0, parts, drain, 0)


def body(n_row, n_col, n_feat, features, tiles, tile_row, tile_col, tile_count, weight, bias):
    side = tiles.shape[-1]
    slots = tiles.shape[2]
    held, width = features.shape
    fan = weight.shape[0]
    hidden = weight.shape[1]
    node_dev = held // n_feat
    brows = n_col * n_feat * node_dev // side
    blocks = held // side
    any_spec = pl.BlockSpec(memory_space=pl.ANY)
    vmem_spec = pl.BlockSpec(memory_space=pltpu.VMEM)
    dma = pltpu.SemaphoreType.DMA

    own = features.reshape(blocks, side, width).transpose(0, 2, 1)
    parts = 4
    sources = pl.pallas_call(
        functools.partial(gather_kernel, n_row, n_feat, parts),
        out_shape=jax.ShapeDtypeStruct((n_row * blocks, fan, side), jnp.bfloat16),
        in_specs=[any_spec],
        out_specs=any_spec,
        scratch_shapes=[
            dma, dma((2, n_feat - 1, parts)), dma((2, n_feat - 1, parts)),
            dma((n_row - 1, n_feat, parts)), dma((n_row - 1, n_feat, parts)),
        ],
        compiler_params=pltpu.CompilerParams(collective_id=0, has_side_effects=True),
        name="gather_sources",
    )(own)

    chunk, unroll = 32, 16
    partial_value = pl.pallas_call(
        functools.partial(tile_kernel, chunk, unroll, brows),
        out_shape=jax.ShapeDtypeStruct((brows, side, fan), jnp.bfloat16),
        grid_spec=pltpu.PrefetchScalarGridSpec(
            num_scalar_prefetch=3,
            grid=(slots // chunk,),
            in_specs=[
                pl.BlockSpec((n_row * blocks, fan, side), lambda i, n, rows, cols: (0, 0, 0), pipeline_mode=pl.Buffered(1)),
                pl.BlockSpec((chunk, side, side), lambda i, n, rows, cols: (jnp.minimum(i, (n[0] - 1) // chunk), 0, 0)),
            ],
            out_specs=any_spec,
            scratch_shapes=[
                pltpu.VMEM((brows + 1, side, fan), jnp.float32),
                pltpu.VMEM((2, 32, side, fan), jnp.bfloat16),
                dma((2,)),
            ],
        ),
        compiler_params=pltpu.CompilerParams(vmem_limit_bytes=60 * MIB),
        name="tile_products",
    )(tile_count.reshape(1), tile_row.reshape(slots), tile_col.reshape(slots), sources, tiles.reshape(slots, side, side))

    size = 128
    parts = node_dev // size
    bf = jnp.bfloat16
    return pl.pallas_call(
        functools.partial(reduce_kernel, n_feat, parts),
        out_shape=jax.ShapeDtypeStruct((node_dev, hidden), bf),
        in_specs=[any_spec, vmem_spec, vmem_spec],
        out_specs=vmem_spec,
        scratch_shapes=[
            pltpu.VMEM((n_feat, node_dev, fan), bf),
            pltpu.VMEM((n_feat, node_dev, fan), bf),
            pltpu.VMEM((parts, n_feat, size, fan), bf),
            pltpu.VMEM((parts, n_feat, size, fan), bf),
            pltpu.VMEM((parts, n_feat, size, fan), bf),
            pltpu.VMEM((parts, n_feat, size, fan), bf),
            pltpu.VMEM((parts, n_feat, size, fan), bf),
            pltpu.VMEM((parts, n_feat - 1, size, fan), bf),
            dma((2,)), dma((parts,)), dma((parts,)), dma((parts,)), dma((parts,)),
            dma((parts,)), dma((parts,)), dma((parts, n_feat - 1)), dma((parts, n_feat - 1)),
        ],
        compiler_params=pltpu.CompilerParams(collective_id=1, has_side_effects=True, vmem_limit_bytes=40 * MIB),
        name="reduce_dense",
    )(partial_value.reshape(n_col // 2, 2, n_feat, node_dev, fan), weight, bias.reshape(1, hidden))


def solution(mesh):
    placed = (
        P(("row", "col"), "feat"),
        P("row", "col", "feat", None, None),
        P("row", "col", "feat"),
        P("row", "col", "feat"),
        P("row", "col", "feat"),
        P(),
        P(),
    )
    shape = mesh.shape
    return jax.shard_map(
        functools.partial(body, shape["row"], shape["col"], shape["feat"]),
        mesh=mesh, in_specs=placed, out_specs=P(("row", "col", "feat"), None), check_vma=False
    )
```
